256 devices in a mesh: ctx: 64 (over z, x, core), head: 4 (over y).
Axes of the slice: x: 4, y: 4, z: 8, core: 2. Of those that a mesh axis runs over, the one named last changes fastest.
Arguments:
- queries: bfloat16 [32768, 3584], P('ctx', 'head'), may hold values from -80 to 80
- keys: bfloat16 [32768, 512], P('ctx', 'head'), may hold values from -4.6 to 4.6
- values: bfloat16 [32768, 512], P('ctx', 'head'), may hold values from -6 to 6
- selection: int32 [256, 12], replicated, may hold values from 0 to 255, as said below
- out_weight: bfloat16 [3584, 3584], P(None, ('head', 'ctx')), may hold values from -1 to 1
Outputs:
- mixed: bfloat16 [32768, 3584], P('ctx', 'head')
The draws below stay inside these ranges and needn't reach their ends.
Inputs may be any that keep to these rules, and one draw needn't show every extreme that they name: `selection`: block b lies on index b // 4 of ctx. Entry 0 of row b is b; the other entries are distinct blocks before b, or b again where fewer than 11 are chosen. The blocks of one index of ctx that the 4 query blocks of another index list number at most 2, and exactly 2 for some pairs of indices.
All inputs are finite; a program needn't handle non-finite values.
Results may differ from the reference program's by a relative error of at most 0.0054.
Values may be sent and summed in bfloat16 or wider, within the bound.
No kernel may reach another device: no remote copies, remote signals or barrier semaphores. Data moves between devices by JAX's collectives and lax.ppermute only.
A program may use at most 128 MiB of HBM per device.

```python
import jax
import jax.numpy as jnp
from jax import lax

D = 3584
QUERY_HEADS = 28
KEY_VALUE_HEADS = 4
HEAD_WIDTH = 128
BLOCK_TOKENS = 128
CHOSEN_BLOCKS = 12
CAP = 2
BLK_DEV = 4
BLOCK_COUNT = 256
TOKEN_COUNT = 32768


def base_keys(key):
    unscaled_logits = jax.random.normal(key, (TOKEN_COUNT, KEY_VALUE_HEADS * HEAD_WIDTH), jnp.float32)
    return jnp.clip(unscaled_logits, -4.0, 4.0)


def draw_keys(key, part):
    first = base_keys(key)
    return first.astype(jnp.bfloat16)


def draw_queries(key, part):
    key = jax.random.fold_in(key, 5)
    return jnp.clip(1.5 * jax.random.normal(key, (TOKEN_COUNT, QUERY_HEADS * HEAD_WIDTH), jnp.float32), -9.0, 9.0).astype(jnp.bfloat16)


def draw_selection(key, part):
    key = jax.random.fold_in(key, 7)
    pool_key, score_key = jax.random.split(key)
    devices = BLOCK_COUNT // BLK_DEV
    block_list = jnp.arange(BLOCK_COUNT, dtype=jnp.int32)
    noise = jax.random.randint(pool_key, (devices, devices, BLK_DEV), 0, 65536) * BLK_DEV + jnp.arange(BLK_DEV, dtype=jnp.int32)
    ranking = jnp.argsort(jnp.argsort(noise, axis=-1), axis=-1)
    pooled = (ranking < CAP).reshape(devices, BLOCK_COUNT)
    query_dev = block_list // BLK_DEV
    query_loc = block_list % BLK_DEV
    remote = (query_dev[None, :] < query_dev[:, None]) & pooled[query_dev]
    local = (query_dev[None, :] == query_dev[:, None]) & (block_list[None, :] < block_list[:, None])
    forced_mask = remote & (query_dev[None, :] == query_dev[:, None] - 1) & (query_loc[:, None] == BLK_DEV - 1)
    score_boost = jnp.where(block_list[None, :] == 0, 131072, 0) + jnp.where(forced_mask, 262144, 0)
    random_scores = jax.random.randint(score_key, (BLOCK_COUNT, BLOCK_COUNT), 0, 65536)
    block_scores = (random_scores + score_boost) * BLOCK_COUNT + block_list[None, :]
    block_scores = jnp.where(remote | local, block_scores, -1)
    top_scores, chosen = lax.top_k(block_scores, CHOSEN_BLOCKS - 1)
    chosen = jnp.where(top_scores >= 0, chosen.astype(jnp.int32), block_list[:, None])
    return jnp.concatenate([block_list[:, None], chosen], axis=1).astype(jnp.int32)


def block_levels(rng, extent, cuts, smallest, largest):
    level, own = 1.0, jax.random.fold_in(rng, 6)
    for dim, shards_of in cuts:
        steps = jnp.exp(jax.random.uniform(jax.random.fold_in(own, dim), (shards_of,), jnp.float32, smallest / len(cuts), largest / len(cuts)))
        level = level * jnp.repeat(steps, extent[dim] // shards_of).reshape([-1 if axis == dim else 1 for axis in range(len(extent))])
    return level


def centred(key, extent, deviation, most, shards=(), kind=jnp.bfloat16):
    loudness = block_levels(key, extent, shards, -0.22, 0.18) if shards else 1.0
    values = jax.random.normal(key, extent, jnp.float32) * deviation * loudness
    return jnp.minimum(jnp.maximum(values, -most), most).astype(kind)


def setup_inputs(seed: int = 0) -> dict:
    seeds = jax.random.split(jax.random.key(seed), 6)
    queries = draw_queries(jax.random.fold_in(seeds[5], 71), 0)
    keys = draw_keys(jax.random.fold_in(seeds[5], 71), 0)
    values = centred(seeds[2], (TOKEN_COUNT, KEY_VALUE_HEADS * HEAD_WIDTH), 1.0, 6.0, ((0, 64), (1, 4)))
    selection = draw_selection(jax.random.fold_in(seeds[5], 71), 0)
    out_weight = centred(seeds[4], (QUERY_HEADS * HEAD_WIDTH, D), (HEAD_WIDTH // 4) ** -0.5, 1.0, ((1, 256),))
    return dict(queries=queries, keys=keys, values=values, selection=selection, out_weight=out_weight)


def attend_block(query_block, gathered_key_rows, gathered_value_rows, filler):
    order = jnp.arange(gathered_key_rows.shape[0])
    entry = order // BLOCK_TOKENS
    within = order % BLOCK_TOKENS
    target = jnp.arange(query_block.shape[0])
    dropped = jnp.any((entry[:, None] == jnp.arange(CHOSEN_BLOCKS)[None, :]) & filler[None, :], axis=1)
    score = jnp.einsum("tkgd,skd->kgts", query_block.astype(jnp.float32), gathered_key_rows.astype(jnp.float32)) * (HEAD_WIDTH ** -0.5)
    visible = jnp.where(entry[None, :] == 0, within[None, :] <= target[:, None], jnp.logical_not(dropped)[None, :])
    score = jnp.where(visible, score, -1e30)
    peak = jnp.max(score, axis=-1, keepdims=True)
    unscaled_logits = jnp.where(visible, jnp.exp(score - peak), 0.0)
    total = jnp.sum(unscaled_logits, axis=-1)
    weight = unscaled_logits.astype(jnp.bfloat16)
    summed = jnp.einsum("kgts,skd->tkgd", weight.astype(jnp.float32), gathered_value_rows.astype(jnp.float32))
    scaled = summed / jnp.transpose(total, (2, 0, 1))[..., None]
    return scaled.astype(jnp.bfloat16).reshape(query_block.shape[0], -1)


def reference(queries, keys, values, selection, out_weight):
    head_group = QUERY_HEADS // KEY_VALUE_HEADS
    blocked_queries = queries.reshape(BLOCK_COUNT, BLOCK_TOKENS, KEY_VALUE_HEADS, head_group, HEAD_WIDTH)
    blocked_keys = keys.reshape(BLOCK_COUNT, BLOCK_TOKENS, KEY_VALUE_HEADS * HEAD_WIDTH)
    blocked_values = values.reshape(BLOCK_COUNT, BLOCK_TOKENS, KEY_VALUE_HEADS * HEAD_WIDTH)

    def attend_one(pieces):
        block_id, query_block, current_row = pieces
        gathered_key_rows = blocked_keys[current_row].reshape(CHOSEN_BLOCKS * BLOCK_TOKENS, KEY_VALUE_HEADS, HEAD_WIDTH)
        gathered_value_rows = blocked_values[current_row].reshape(CHOSEN_BLOCKS * BLOCK_TOKENS, KEY_VALUE_HEADS, HEAD_WIDTH)
        filler = (current_row == block_id) & (jnp.arange(CHOSEN_BLOCKS) > 0)
        return attend_block(query_block, gathered_key_rows, gathered_value_rows, filler)

    attended = lax.map(attend_one, (jnp.arange(BLOCK_COUNT, dtype=jnp.int32), blocked_queries, selection))

    def project(rows):
        return jnp.dot(rows, out_weight, preferred_element_type=jnp.float32).astype(jnp.bfloat16)

    mixed = lax.map(project, attended)
    return mixed.reshape(TOKEN_COUNT, D)
```

```python
import functools
import math

import jax
import jax.numpy as jnp
from jax import lax
from jax.experimental import pallas as pl
from jax.experimental.pallas import tpu as pltpu
from jax.sharding import PartitionSpec as P

HEAD = 128
BLOCK = 128
CHOSEN = 12
NZ, NX = 8, 4
MASKED = -1e30


def shift(a, dz=0, dx=0, dc=0):
    pairs = []
    for z in range(NZ):
        for x in range(NX):
            for c in range(2):
                to = ((z + dz) % NZ) * 2 * NX + ((x + dx) % NX) * 2 + (c + dc) % 2
                pairs.append((z * 2 * NX + x * 2 + c, to))
    return lax.ppermute(a, "ctx", pairs)


def over_head(a, step):
    return lax.ppermute(a, "head", [(i, (i + step) % 4) for i in range(4)])


def gather_x_first(own):
    n = own.shape[0]
    r1, l1 = shift(own, dx=1), shift(own, dx=-1)
    r2, l2 = shift(r1[: n // 2], dx=1), shift(l1[n // 2 :], dx=-1)
    row = jnp.concatenate([own, r1, l1, r2, l2], axis=0)
    m = row.shape[0]
    u1, d1 = shift(row, dz=1), shift(row, dz=-1)
    u2, d2 = shift(u1, dz=1), shift(d1, dz=-1)
    u3, d3 = shift(u2, dz=1), shift(d2, dz=-1)
    u4, d4 = shift(u3[: m // 2], dz=1), shift(d3[m // 2 :], dz=-1)
    return [row, u1, d1, u2, d2, u3, d3, u4, d4]


def gather_z_first(own):
    n = own.shape[0]
    u1, d1 = shift(own, dz=1), shift(own, dz=-1)
    u2, d2 = shift(u1, dz=1), shift(d1, dz=-1)
    u3, d3 = shift(u2, dz=1), shift(d2, dz=-1)
    u4, d4 = shift(u3[: n // 2], dz=1), shift(d3[n // 2 :], dz=-1)
    column = jnp.concatenate([own, u1, d1, u2, d2, u3, d3, u4, d4], axis=0)
    m = column.shape[0]
    r1, l1 = shift(column, dx=1), shift(column, dx=-1)
    r2, l2 = shift(r1[: m // 2], dx=1), shift(l1[m // 2 :], dx=-1)
    return [column, r1, l1, r2, l2]


def pick(index, options):
    out = jnp.int32(options[0])
    for k, option in enumerate(options[1:], 1):
        out = jnp.where(index == k, jnp.int32(option), out)
    return out


def locate(me, block):
    source, local = block >> 2, block & 3
    dz = ((source >> 3) - (me >> 3)) & 7
    dx = ((source >> 1) - (me >> 1)) & 3
    other_core = (source ^ me) & 1
    in_x_first = local < 2
    x_slot = pick(dx, [0, 2, 3, 1])
    z_slot = pick(dz, [0, 2, 4, 6, 7, 5, 3, 1])
    far_z, far_x = dz == 4, dx == 2
    a_buffer = jnp.where(far_z, 7 + (x_slot >> 1), pick(dz, [0, 2, 4, 6, 7, 5, 3, 1]))
    a_unit = jnp.where(far_z, x_slot & 1, x_slot)
    b_buffer = jnp.where(far_x, 3 + (z_slot >> 2), pick(dx, [0, 2, 3, 1]))
    b_unit = jnp.where(far_x, z_slot & 3, z_slot)
    buffer = jnp.where(in_x_first, a_buffer, 9 + b_buffer) + 14 * other_core
    unit = jnp.where(in_x_first, a_unit, b_unit)
    return buffer, unit * 512 + (local & 1) * BLOCK


def attend_kernel(rows_ref, me_ref, q_ref, *rest):
    tables, (out_ref, k_buf, v_buf, sem) = rest[:28], rest[28:]
    step, steps = pl.program_id(0), pl.num_programs(0)
    me = me_ref[0]

    def fetch(i, slot):
        def one(j, carry):
            block = rows_ref[i, j]
            buffer, row = locate(me, block)
            to = pl.multiple_of(j * BLOCK, BLOCK)

            def start(table):
                k_row = pl.multiple_of(row, BLOCK)
                v_row = pl.multiple_of(row + 2 * BLOCK, BLOCK)
                pltpu.make_async_copy(
                    table.at[pl.ds(k_row, BLOCK), :], k_buf.at[slot, pl.ds(to, BLOCK), :], sem.at[slot]
                ).start()
                pltpu.make_async_copy(
                    table.at[pl.ds(v_row, BLOCK), :],
                    v_buf.at[slot, pl.ds(to, BLOCK), pl.ds(0, HEAD)],
                    sem.at[slot],
                ).start()

            for t, table in enumerate(tables):
                pl.when(buffer == t)(functools.partial(start, table))
            return carry

        lax.fori_loop(0, CHOSEN, one, 0)

    @pl.when(step == 0)
    def _():
        v_buf[:, :, HEAD:] = jnp.ones((2, CHOSEN * BLOCK, HEAD), jnp.bfloat16)
        fetch(0, 0)

    @pl.when(step + 1 < steps)
    def _():
        fetch(step + 1, (step + 1) & 1)

    slot = step & 1
    own_block = me * steps + step
    biases = [None] + [
        jnp.where(rows_ref[step, j] == own_block, jnp.float32(MASKED), jnp.float32(0.0))
        for j in range(1, CHOSEN)
    ]
    pltpu.make_async_copy(v_buf.at[slot], v_buf.at[slot], sem.at[slot]).wait()
    token = lax.broadcasted_iota(jnp.int32, (BLOCK, BLOCK), 0)
    key = lax.broadcasted_iota(jnp.int32, (BLOCK, BLOCK), 1)
    causal = key <= token
    factor = jnp.float32(HEAD**-0.5 * math.log2(math.e))
    k_all = k_buf[slot]
    v_all = v_buf[slot]
    for g in range(q_ref.shape[1] // HEAD):
        q = q_ref[:, g * HEAD : (g + 1) * HEAD]
        s = lax.dot_general(q, k_all, (((1,), (1,)), ((), ())), preferred_element_type=jnp.float32)
        parts = [jnp.where(causal, s[:, :BLOCK], MASKED)]
        for j in range(1, CHOSEN):
            parts.append(s[:, j * BLOCK : (j + 1) * BLOCK] + biases[j])
        top = parts[0]
        for part in parts[1:]:
            top = jnp.maximum(top, part)
        peak = jnp.max(top, axis=1, keepdims=True)
        weight = jnp.concatenate(
            [jnp.exp2((part - peak) * factor).astype(jnp.bfloat16) for part in parts], axis=1
        )
        o = jnp.dot(weight, v_all, preferred_element_type=jnp.float32)
        out_ref[:, g * HEAD : (g + 1) * HEAD] = (o[:, :HEAD] / o[:, HEAD:]).astype(jnp.bfloat16)


def attend(rows, me, queries, tables):
    tokens, width = queries.shape
    steps = tokens // BLOCK
    spec = pl.BlockSpec((BLOCK, width), lambda i, *_: (i, 0))
    return pl.pallas_call(
        attend_kernel,
        grid_spec=pltpu.PrefetchScalarGridSpec(
            num_scalar_prefetch=2,
            grid=(steps,),
            in_specs=[spec] + [pl.BlockSpec(memory_space=pl.ANY)] * len(tables),
            out_specs=spec,
            scratch_shapes=[
                pltpu.VMEM((2, CHOSEN * BLOCK, HEAD), jnp.bfloat16),
                pltpu.VMEM((2, CHOSEN * BLOCK, 2 * HEAD), jnp.bfloat16),
                pltpu.SemaphoreType.DMA((2,)),
            ],
        ),
        out_shape=jax.ShapeDtypeStruct((tokens, width), jnp.bfloat16),
        compiler_params=pltpu.CompilerParams(vmem_limit_bytes=24 * 1024 * 1024),
        cost_estimate=pl.CostEstimate(flops=3 * 10**9, bytes_accessed=8 * 10**6, transcendentals=5 * 10**6),
        name="attend",
    )(rows, me, queries, *tables)


def project_kernel(heads_ref, a0, a1, a2, a3, w_ref, sel_ref, out_ref, acc_ref):
    step = pl.program_id(0)
    for r, a in enumerate((a0, a1, a2, a3)):

        @pl.when(step == r)
        def _(r=r, a=a):
            term = lax.dot_general(
                a[...], w_ref[...], (((1,), (1,)), ((), ())), preferred_element_type=jnp.float32
            )
            if r == 0:
                acc_ref[...] = term
            elif r < 3:
                acc_ref[...] += term
            else:
                padded = (acc_ref[...] + term).astype(jnp.bfloat16)
                out_ref[...] = jnp.dot(
                    padded, sel_ref[...], preferred_element_type=jnp.float32
                ).astype(jnp.bfloat16)


def project(heads, attended, weight_rows, sel):
    tokens, width = attended[0].shape
    padded = weight_rows.shape[0]
    whole = pl.BlockSpec((tokens, width), lambda r, *_: (0, 0))
    return pl.pallas_call(
        project_kernel,
        grid_spec=pltpu.PrefetchScalarGridSpec(
            num_scalar_prefetch=1,
            grid=(4,),
            in_specs=[whole] * 4
            + [
                pl.BlockSpec((padded, width), lambda r, heads: (0, heads[r])),
                pl.BlockSpec(sel.shape, lambda r, *_: (0, 0)),
            ],
            out_specs=pl.BlockSpec((tokens, sel.shape[1]), lambda r, *_: (0, 0)),
            scratch_shapes=[pltpu.VMEM((tokens, padded), jnp.float32)],
        ),
        out_shape=jax.ShapeDtypeStruct((tokens, sel.shape[1]), jnp.bfloat16),
        compiler_params=pltpu.CompilerParams(vmem_limit_bytes=32 * 1024 * 1024),
        cost_estimate=pl.CostEstimate(flops=4 * 10**9, bytes_accessed=12 * 10**6, transcendentals=0),
        name="project",
    )(heads, *attended, weight_rows, sel)


def per_device(queries, keys, values, selection, out_weight):
    me = lax.axis_index("ctx")
    y = lax.axis_index("head")
    half = keys.shape[0] // 2
    first = jnp.concatenate([keys[:half], values[:half]], axis=0)
    second = jnp.concatenate([keys[half:], values[half:]], axis=0)
    tables = gather_x_first(first) + gather_z_first(second)
    tables = tables + [shift(t, dc=1) for t in tables]
    columns = out_weight.shape[1]
    weight_rows = lax.all_gather(
        jnp.pad(out_weight.T, ((0, 16 - columns), (0, 0))), "ctx", axis=0, tiled=True
    )
    blocks_here = keys.shape[0] // BLOCK
    rows = lax.dynamic_slice_in_dim(selection, me * blocks_here, blocks_here, 0)
    attended = attend(rows, me.reshape(1), queries, tables)
    up, down = over_head(attended, 1), over_head(attended, -1)
    h = attended.shape[0] // 2
    far = jnp.concatenate([over_head(up[:h], 1), over_head(down[h:], -1)], axis=0)
    heads = jnp.stack([y, (y + 3) % 4, (y + 1) % 4, (y + 2) % 4]).astype(jnp.int32)
    padded = lax.broadcasted_iota(jnp.int32, (weight_rows.shape[0], 64 * columns), 0)
    column = lax.broadcasted_iota(jnp.int32, padded.shape, 1)
    sel = ((padded // 16) * columns + padded % 16 == column) & (padded % 16 < columns)
    return project(heads, [attended, up, down, far], weight_rows, sel.astype(jnp.bfloat16))


def solution(mesh):
    placed = (P("ctx", "head"), P("ctx", "head"), P("ctx", "head"), P(), P(None, ("head", "ctx")))
    return jax.shard_map(
        per_device, mesh=mesh, in_specs=placed, out_specs=P("ctx", "head"), check_vma=False
    )
```

```python
import functools
import math

import jax
import jax.numpy as jnp
from jax import lax
from jax.experimental import pallas as pl
from jax.experimental.pallas import tpu as pltpu
from jax.sharding import PartitionSpec as P

HEAD = 128
BLOCK = 128
CHOSEN = 12
BLK_DEV = 4
IN_A = 3
NZ, NX = 8, 4
MASKED = -1e30
TABLES = pl.ANY
VMEM_GRANT = 60 * 1024 * 1024


def along(hop):
    pairs = []
    for z in range(NZ):
        for x in range(NX):
            for c in range(2):
                to_z, to_x, to_c = hop(z, x, c, 1 - 2 * c)
                to = (to_z % NZ) * 2 * NX + (to_x % NX) * 2 + to_c
                pairs.append((z * 2 * NX + x * 2 + c, to))
    return pairs


def next_z(a):
    return lax.ppermute(a, "ctx", along(lambda z, x, c, way: (z + way, x, c)))


def next_x(a):
    return lax.ppermute(a, "ctx", along(lambda z, x, c, way: (z, x + way, c)))


def swap(a):
    return lax.ppermute(a, "ctx", along(lambda z, x, c, way: (z, x, 1 - c)))


def over_head(a, step):
    return lax.ppermute(a, "head", [(i, (i + step) % 4) for i in range(4)])


def join(*parts):
    return jnp.concatenate(parts, axis=0)


def after(a, *others):
    return lax.optimization_barrier((a, *others))[0]


def both_cores(u, mine, theirs, far, far_theirs, own, other):
    same = [own] + [t[:u] for t in mine] + [far] + [t[u:] for t in reversed(theirs)]
    cross = [other] + [t[u:] for t in mine] + [far_theirs] + [t[:u] for t in reversed(theirs)]
    return same, cross


def row_of(x1, x2, swapped, own, other):
    u = own.shape[0]
    same, cross = both_cores(u, [x1], [swapped[: 2 * u]], x2, swapped[2 * u :], own, other)
    return join(*same, *cross)


def gather(a_own, a_other, b_own, b_other, w_own, w_other):
    u, n, v = a_own.shape[0], b_own.shape[0], w_own.shape[0]
    bz1 = next_z(join(b_own, b_other))
    bz1s = swap(bz1)
    bz2 = next_z(bz1)
    ax1 = next_x(after(join(a_own, a_other), bz1))
    near = join(b_own, bz1[:n], bz1s[n:], b_other, bz1[n:], bz1s[:n])
    bz3 = next_z(after(bz2, ax1))
    ax2 = next_x(after(ax1[:u], bz2))
    bx1n = next_x(after(near, bz2))
    wx1 = next_x(after(join(w_own, w_other), bz2))
    row = row_of(ax1, ax2, swap(join(ax1, ax2)), a_own, a_other)
    bz4 = next_z(after(bz3, ax2)[:n])
    az1 = next_z(after(row, bz3))
    bzs = swap(after(join(bz2, bz3, bz4), bx1n))
    theirs = [bzs[: 2 * n], bzs[2 * n : 4 * n]]
    same, cross = both_cores(n, [bz2, bz3], theirs, bz4, bzs[4 * n :], b_own, b_other)
    rest_same, rest_cross = join(*same[1:]), join(*cross[1:])
    rest_same = after(rest_same, az1)
    bx1s = next_x(rest_same)
    bx2n = next_x(after(bx1n, az1)[: 3 * n])
    az2 = next_z(az1)
    wx2 = next_x(after(wx1, az1)[:v])
    az3 = next_z(after(az2, bx1s, bx2n))
    bx1c = next_x(after(rest_cross, az2))
    bx2r = next_x(bx1s)
    w_row = row_of(wx1, wx2, swap(join(wx1, wx2)), w_own, w_other)
    az4 = next_z(az3[: 4 * u])
    tables = [row, az1, az2, az3, az4] + [swap(t) for t in (az1, az2, az3, az4)]
    tables += [near, bx1n, bx2n, swap(bx1n), swap(bx2n)]
    tables += [rest_same, bx1s, bx2r, swap(bx1s), swap(bx2r)]
    tables += [rest_cross, bx1c, swap(bx1c)]
    return tables, after(w_row, az3)


def relative(me, source, core):
    dz, dx = (me >> 3) - (source >> 3), (me >> 1) - (source >> 1)
    way = 1 - 2 * core
    return (way * dz) & 7, (way * dx) & 3, (source ^ core) & 1


def locate(me, block):
    source, local = block >> 2, block & 3
    core = me & 1
    dz, dx, cross = relative(me, source, core)
    dz_s, dx_s, cross_s = relative(me, source, 1 - core)
    a_mine = (dz < 4) | ((dz == 4) & (cross == 0))
    a_buffer = jnp.where(a_mine, dz, 4 + dz_s)
    a_unit = jnp.where(a_mine, cross * 4 + dx, cross_s * 4 + dx_s)
    b_mine = (dx < 2) | ((dx == 2) & (cross == 0))
    steps = jnp.where(b_mine, dz, dz_s)
    across = jnp.where(b_mine, cross, cross_s)
    hop = jnp.where(b_mine, dx, dx_s)
    near = (steps < 2) | (steps == 7)
    full = jnp.where(b_mine, hop, 2 + hop)
    short = 19 + jnp.where(b_mine, hop, 1 + hop)
    b_buffer = jnp.where(near, 9 + full, jnp.where(across == 0, 14 + full, short))
    b_unit = jnp.where(near, across * 3 + jnp.where(steps == 7, 2, steps), steps - 2)
    a_row, b_row = a_unit * (IN_A * BLOCK), b_unit * ((2 * BLK_DEV - IN_A) * BLOCK)

    def place(piece):
        first = piece < IN_A
        return (
            jnp.where(first, a_buffer, b_buffer),
            jnp.where(first, a_row + piece * BLOCK, b_row + (piece - IN_A) * BLOCK),
        )

    return place(local), place(BLK_DEV + local)


def attend_kernel(first, rows_ref, me_ref, q_ref, *rest):
    tables, (out_ref, k_buf, v_buf, sem) = rest[:22], rest[22:]
    step, steps = pl.program_id(0), pl.num_programs(0)
    me = me_ref[0]

    def fetch(i, slot):
        def one(j, carry):
            block = rows_ref[first + i, j]
            (k_table, k_row), (v_table, v_row) = locate(me, block)
            to = pl.multiple_of(j * BLOCK, BLOCK)
            k_row, v_row = pl.multiple_of(k_row, BLOCK), pl.multiple_of(v_row, BLOCK)
            k_to = k_buf.at[slot, pl.ds(to, BLOCK), :]
            v_to = v_buf.at[slot, pl.ds(to, BLOCK), pl.ds(0, HEAD)]

            def start(table, row, target):
                pltpu.make_async_copy(table.at[pl.ds(row, BLOCK), :], target, sem.at[slot]).start()

            for t, table in enumerate(tables):
                pl.when(k_table == t)(functools.partial(start, table, k_row, k_to))
                pl.when(v_table == t)(functools.partial(start, table, v_row, v_to))
            return carry

        lax.fori_loop(0, CHOSEN, one, 0)

    @pl.when(step == 0)
    def _():
        v_buf[:, :, HEAD:] = jnp.ones((2, CHOSEN * BLOCK, HEAD), jnp.bfloat16)
        fetch(0, 0)

    @pl.when(step + 1 < steps)
    def _():
        fetch(step + 1, (step + 1) & 1)

    slot = step & 1
    own_block = me * rows_ref.shape[0] + first + step
    biases = [None] + [
        jnp.where(rows_ref[first + step, j] == own_block, jnp.float32(MASKED), jnp.float32(0.0))
        for j in range(1, CHOSEN)
    ]
    pltpu.make_async_copy(v_buf.at[slot], v_buf.at[slot], sem.at[slot]).wait()
    token = lax.broadcasted_iota(jnp.int32, (BLOCK, BLOCK), 0)
    key = lax.broadcasted_iota(jnp.int32, (BLOCK, BLOCK), 1)
    causal = key <= token
    factor = jnp.float32(HEAD**-0.5 * math.log2(math.e))
    k_all = k_buf[slot]
    v_all = v_buf[slot]
    for g in range(q_ref.shape[1] // HEAD):
        q = q_ref[:, g * HEAD : (g + 1) * HEAD]
        s = lax.dot_general(q, k_all, (((1,), (1,)), ((), ())), preferred_element_type=jnp.float32)
        parts = [jnp.where(causal, s[:, :BLOCK], MASKED)]
        for j in range(1, CHOSEN):
            parts.append(s[:, j * BLOCK : (j + 1) * BLOCK] + biases[j])
        top = parts[0]
        for part in parts[1:]:
            top = jnp.maximum(top, part)
        peak = jnp.max(top, axis=1, keepdims=True)
        weight = jnp.concatenate(
            [jnp.exp2((part - peak) * factor).astype(jnp.bfloat16) for part in parts], axis=1
        )
        o = jnp.dot(weight, v_all, preferred_element_type=jnp.float32)
        out_ref[:, g * HEAD : (g + 1) * HEAD] = (o[:, :HEAD] / o[:, HEAD:]).astype(jnp.bfloat16)


def attend(rows, me, queries, tables, first, steps):
    width = queries.shape[1]
    tokens = steps * BLOCK
    spec = pl.BlockSpec((BLOCK, width), lambda i, *_: (first + i, 0))
    return pl.pallas_call(
        functools.partial(attend_kernel, first),
        grid_spec=pltpu.PrefetchScalarGridSpec(
            num_scalar_prefetch=2,
            grid=(steps,),
            in_specs=[spec] + [pl.BlockSpec(memory_space=TABLES)] * len(tables),
            out_specs=pl.BlockSpec((BLOCK, width), lambda i, *_: (i, 0)),
            scratch_shapes=[
                pltpu.VMEM((2, CHOSEN * BLOCK, HEAD), jnp.bfloat16),
                pltpu.VMEM((2, CHOSEN * BLOCK, 2 * HEAD), jnp.bfloat16),
                pltpu.SemaphoreType.DMA((2,)),
            ],
        ),
        out_shape=jax.ShapeDtypeStruct((tokens, width), jnp.bfloat16),
        compiler_params=pltpu.CompilerParams(vmem_limit_bytes=VMEM_GRANT),
        cost_estimate=pl.CostEstimate(flops=3 * 10**9, bytes_accessed=8 * 10**6, transcendentals=5 * 10**6),
        name="attend%d" % first,
    )(rows, me, queries, *tables)


def project_kernel(heads_ref, *refs):
    attended, (sel_ref, *weights), (out_ref, acc_ref, w_buf, sem) = refs[:10], refs[10:-4], refs[-4:]
    width = w_buf.shape[2]

    def fetch(r):
        column = pl.multiple_of(heads_ref[r] * width, width)
        start = 0
        for w in weights:
            n = w.shape[0]
            to = w_buf.at[r % 2, pl.ds(start, n), :]
            pltpu.make_async_copy(w.at[:, pl.ds(column, width)], to, sem.at[r % 2]).start()
            start += n

    fetch(0)
    for r in range(4):
        if r < 3:
            fetch(r + 1)
            a = jnp.concatenate([t[...] for t in attended[2 * r : 2 * r + 2]], axis=0)
        else:
            a = jnp.concatenate([t[...] for t in attended[6:]], axis=0)
        whole = w_buf.at[r % 2]
        pltpu.make_async_copy(whole, whole, sem.at[r % 2]).wait()
        term = lax.dot_general(
            a, w_buf[r % 2], (((1,), (1,)), ((), ())), preferred_element_type=jnp.float32
        )
        if r == 0:
            acc_ref[...] = term
        else:
            acc_ref[...] += term
    out_ref[...] = jnp.dot(
        acc_ref[...].astype(jnp.bfloat16), sel_ref[...], preferred_element_type=jnp.float32
    ).astype(jnp.bfloat16)


def project(heads, attended, weights, sel):
    width = attended[0].shape[1]
    tokens = attended[0].shape[0] + attended[1].shape[0]
    padded = sum(w.shape[0] for w in weights)
    vmem = pl.BlockSpec(memory_space=pltpu.VMEM)
    return pl.pallas_call(
        project_kernel,
        in_specs=[pl.BlockSpec(memory_space=pltpu.SMEM)]
        + [vmem] * (len(attended) + 1)
        + [pl.BlockSpec(memory_space=pl.ANY)] * len(weights),
        out_specs=vmem,
        scratch_shapes=[
            pltpu.VMEM((tokens, padded), jnp.float32),
            pltpu.VMEM((2, padded, width), jnp.bfloat16),
            pltpu.SemaphoreType.DMA((2,)),
        ],
        out_shape=jax.ShapeDtypeStruct((tokens, sel.shape[1]), jnp.bfloat16),
        compiler_params=pltpu.CompilerParams(vmem_limit_bytes=VMEM_GRANT),
        cost_estimate=pl.CostEstimate(flops=4 * 10**9, bytes_accessed=14 * 10**6, transcendentals=0),
        name="project",
    )(heads, *attended, sel, *weights)


def unit_sources(me):
    core = me & 1
    z, x = me >> 3, (me >> 1) & 3
    unit = jnp.arange(64)
    dz = jnp.where(unit < 36, unit // 8, (unit - 36) // 8 + 1)
    slot = jnp.where(unit < 36, unit % 8, (unit - 36) % 8)
    holder = jnp.where(unit < 36, core, 1 - core)
    way = 1 - 2 * holder
    from_z = (z - way * dz) & 7
    from_x = (x - way * (slot & 3)) & 3
    return from_z * 8 + from_x * 2 + (holder ^ (slot >> 2))


def per_device(queries, keys, values, selection, out_weight):
    me = lax.axis_index("ctx")
    y = lax.axis_index("head")
    own = join(keys, values)
    other = swap(own)
    columns = out_weight.shape[1]
    own_rows = jnp.pad(out_weight.T, ((0, 16 - columns), (0, 0)))
    n = IN_A * BLOCK
    tables, w_row = gather(own[:n], other[:n], own[n:], other[n:], own_rows, swap(own_rows))
    blocks_here = keys.shape[0] // BLOCK
    rows = lax.dynamic_slice_in_dim(selection, me * blocks_here, blocks_here, 0)
    heads = jnp.stack([y, (y + 3) % 4, (y + 1) % 4, (y + 2) % 4]).astype(jnp.int32)
    target = unit_sources(me)[:, None] * columns + jnp.arange(16)[None, :]
    target = jnp.where(jnp.arange(16)[None, :] < columns, target, -1).reshape(-1)
    sel = (target[:, None] == jnp.arange(64 * columns)[None, :]).astype(jnp.bfloat16)
    first, second = [attend(rows, me.reshape(1), queries, tables, i, 2) for i in (0, 2)]
    weights = [w_row]
    for i in range(4):
        weights.append(next_z(weights[-1] if i < 3 else weights[-1][: weights[-1].shape[0] // 2]))
    weights += [swap(w) for w in weights[1:]]
    ups, downs = [over_head(first, 1)], [over_head(first, -1)]
    ups[0], downs[0], second = lax.optimization_barrier((ups[0], downs[0], second))
    ups.append(over_head(second, 1))
    downs.append(over_head(second, -1))
    h = first.shape[0] // 2
    far = []
    for up, down in zip(ups, downs):
        far += [over_head(up[:h], 1), over_head(down[h:], -1)]
    return project(heads, [first, second, *ups, *downs, *far], weights, sel)


def solution(mesh):
    placed = (P("ctx", "head"), P("ctx", "head"), P("ctx", "head"), P(), P(None, ("head", "ctx")))
    return jax.shard_map(
        per_device, mesh=mesh, in_specs=placed, out_specs=P("ctx", "head"), check_vma=False
    )
```

```python
import functools
import math

import jax
import jax.numpy as jnp
from jax import lax
from jax.experimental import pallas as pl
from jax.experimental.pallas import tpu as pltpu
from jax.sharding import PartitionSpec as P

HEAD = 128
BLOCK = 128
CHOSEN = 12
BLK_DEV = 4
IN_A = 3
NZ, NX = 8, 4
MASKED = -1e30
TABLES = pl.ANY
VMEM_GRANT = 60 * 1024 * 1024


def along(hop):
    pairs = []
    for z in range(NZ):
        for x in range(NX):
            for c in range(2):
                to_z, to_x, to_c = hop(z, x, c, 1 - 2 * c)
                to = (to_z % NZ) * 2 * NX + (to_x % NX) * 2 + to_c
                pairs.append((z * 2 * NX + x * 2 + c, to))
    return pairs


def next_z(a):
    return lax.ppermute(a, "ctx", along(lambda z, x, c, way: (z + way, x, c)))


def next_x(a):
    return lax.ppermute(a, "ctx", along(lambda z, x, c, way: (z, x + way, c)))


def swap(a):
    return lax.ppermute(a, "ctx", along(lambda z, x, c, way: (z, x, 1 - c)))


def over_head(a, step):
    return lax.ppermute(a, "head", [(i, (i + step) % 4) for i in range(4)])


def join(*parts):
    return jnp.concatenate(parts, axis=0)


def after(a, *others):
    return lax.optimization_barrier((a, *others))[0]


def both_cores(u, mine, theirs, far, far_theirs, own, other):
    same = [own] + [t[:u] for t in mine] + [far] + [t[u:] for t in reversed(theirs)]
    cross = [other] + [t[u:] for t in mine] + [far_theirs] + [t[:u] for t in reversed(theirs)]
    return same, cross


def row_of(x1, x2, swapped, own, other):
    u = own.shape[0]
    same, cross = both_cores(u, [x1], [swapped[: 2 * u]], x2, swapped[2 * u :], own, other)
    return join(*same, *cross)


def gather(a_own, a_other, b_own, b_other, w_own, w_other):
    u, n, v = a_own.shape[0], b_own.shape[0], w_own.shape[0]
    bz1 = next_z(join(b_own, b_other))
    bz1s = swap(bz1)
    bz2 = next_z(bz1)
    ax1 = next_x(after(join(a_own, a_other), bz1))
    wx1 = next_x(after(join(w_own, w_other), bz1))
    near = join(b_own, bz1[:n], bz1s[n:], b_other, bz1[n:], bz1s[:n])
    bz3 = next_z(after(bz2, ax1))
    ax2 = next_x(after(ax1[:u], bz2))
    bx1n = next_x(after(near, bz2))
    row = row_of(ax1, ax2, swap(join(ax1, ax2)), a_own, a_other)
    bz4 = next_z(after(bz3, ax2, wx1)[:n])
    wx2 = next_x(after(wx1, bz3)[:v])
    az1 = next_z(after(row, bz3))
    bx2n = next_x(after(bx1n, bz3)[: 3 * n])
    bzs = swap(join(bz2, bz3, bz4))
    theirs = [bzs[: 2 * n], bzs[2 * n : 4 * n]]
    same, cross = both_cores(n, [bz2, bz3], theirs, bz4, bzs[4 * n :], b_own, b_other)
    rest_same, rest_cross = join(*same[1:]), join(*cross[1:])
    rest_same = after(rest_same, az1, wx2)
    bx1s, az2 = next_x(rest_same), next_z(az1)
    wxs = swap(after(join(wx1, wx2), az1))
    az2, bx1s, bx2n, wxs = lax.optimization_barrier((az2, bx1s, bx2n, wxs))
    bx1c, az3 = next_x(after(rest_cross, az2)), next_z(az2)
    az3, bx1c = lax.optimization_barrier((az3, bx1c))
    bx2r, az4 = next_x(after(bx1s, az3)), next_z(az3[: 4 * u])
    w_row = row_of(wx1, wx2, wxs, w_own, w_other)
    az4s = swap(az4)
    tables = [row, az1, az2, az3, az4, swap(az1), swap(az2), swap(az3), az4s]
    tables += [near, bx1n, bx2n, swap(bx1n), swap(bx2n)]
    tables += [rest_same, bx1s, bx2r, swap(bx1s), swap(after(bx2r, az4s))]
    tables += [rest_cross, bx1c, swap(bx1c)]
    return tables, next_z(after(w_row, az4s)), w_row


def relative(me, source, core):
    dz, dx = (me >> 3) - (source >> 3), (me >> 1) - (source >> 1)
    way = 1 - 2 * core
    return (way * dz) & 7, (way * dx) & 3, (source ^ core) & 1


def locate(me, block):
    source, local = block >> 2, block & 3
    core = me & 1
    dz, dx, cross = relative(me, source, core)
    dz_s, dx_s, cross_s = relative(me, source, 1 - core)
    a_mine = (dz < 4) | ((dz == 4) & (cross == 0))
    a_buffer = jnp.where(a_mine, dz, 4 + dz_s)
    a_unit = jnp.where(a_mine, cross * 4 + dx, cross_s * 4 + dx_s)
    b_mine = (dx < 2) | ((dx == 2) & (cross == 0))
    steps = jnp.where(b_mine, dz, dz_s)
    across = jnp.where(b_mine, cross, cross_s)
    hop = jnp.where(b_mine, dx, dx_s)
    near = (steps < 2) | (steps == 7)
    full = jnp.where(b_mine, hop, 2 + hop)
    short = 19 + jnp.where(b_mine, hop, 1 + hop)
    b_buffer = jnp.where(near, 9 + full, jnp.where(across == 0, 14 + full, short))
    b_unit = jnp.where(near, across * 3 + jnp.where(steps == 7, 2, steps), steps - 2)
    a_row, b_row = a_unit * (IN_A * BLOCK), b_unit * ((2 * BLK_DEV - IN_A) * BLOCK)

    def place(piece):
        first = piece < IN_A
        return (
            jnp.where(first, a_buffer, b_buffer),
            jnp.where(first, a_row + piece * BLOCK, b_row + (piece - IN_A) * BLOCK),
        )

    return place(local), place(BLK_DEV + local)


def attend_kernel(first, rows_ref, me_ref, q_ref, *rest):
    tables, (out_ref, k_buf, v_buf, sem) = rest[:22], rest[22:]
    step, steps = pl.program_id(0), pl.num_programs(0)
    me = me_ref[0]

    def fetch(i, slot):
        def one(j, carry):
            block = rows_ref[first + i, j]
            (k_table, k_row), (v_table, v_row) = locate(me, block)
            to = pl.multiple_of(j * BLOCK, BLOCK)
            k_row, v_row = pl.multiple_of(k_row, BLOCK), pl.multiple_of(v_row, BLOCK)
            k_to = k_buf.at[slot, pl.ds(to, BLOCK), :]
            v_to = v_buf.at[slot, pl.ds(to, BLOCK), pl.ds(0, HEAD)]

            def start(table, row, target):
                pltpu.make_async_copy(table.at[pl.ds(row, BLOCK), :], target, sem.at[slot]).start()

            for t, table in enumerate(tables):
                pl.when(k_table == t)(functools.partial(start, table, k_row, k_to))
                pl.when(v_table == t)(functools.partial(start, table, v_row, v_to))
            return carry

        lax.fori_loop(0, CHOSEN, one, 0)

    @pl.when(step == 0)
    def _():
        v_buf[:, :, HEAD:] = jnp.ones((2, CHOSEN * BLOCK, HEAD), jnp.bfloat16)
        fetch(0, 0)

    @pl.when(step + 1 < steps)
    def _():
        fetch(step + 1, (step + 1) & 1)

    slot = step & 1
    own_block = me * rows_ref.shape[0] + first + step
    biases = [None] + [
        jnp.where(rows_ref[first + step, j] == own_block, jnp.float32(MASKED), jnp.float32(0.0))
        for j in range(1, CHOSEN)
    ]
    pltpu.make_async_copy(v_buf.at[slot], v_buf.at[slot], sem.at[slot]).wait()
    token = lax.broadcasted_iota(jnp.int32, (BLOCK, BLOCK), 0)
    key = lax.broadcasted_iota(jnp.int32, (BLOCK, BLOCK), 1)
    causal = key <= token
    factor = jnp.float32(HEAD**-0.5 * math.log2(math.e))
    k_all = k_buf[slot]
    v_all = v_buf[slot]
    for g in range(q_ref.shape[1] // HEAD):
        q = q_ref[:, g * HEAD : (g + 1) * HEAD]
        s = lax.dot_general(q, k_all, (((1,), (1,)), ((), ())), preferred_element_type=jnp.float32)
        parts = [jnp.where(causal, s[:, :BLOCK], MASKED)]
        for j in range(1, CHOSEN):
            parts.append(s[:, j * BLOCK : (j + 1) * BLOCK] + biases[j])
        top = parts[0]
        for part in parts[1:]:
            top = jnp.maximum(top, part)
        peak = jnp.max(top, axis=1, keepdims=True)
        weight = jnp.concatenate(
            [jnp.exp2((part - peak) * factor).astype(jnp.bfloat16) for part in parts], axis=1
        )
        o = jnp.dot(weight, v_all, preferred_element_type=jnp.float32)
        out_ref[:, g * HEAD : (g + 1) * HEAD] = (o[:, :HEAD] / o[:, HEAD:]).astype(jnp.bfloat16)


def attend(rows, me, queries, tables, first, steps):
    width = queries.shape[1]
    tokens = steps * BLOCK
    spec = pl.BlockSpec((BLOCK, width), lambda i, *_: (first + i, 0))
    return pl.pallas_call(
        functools.partial(attend_kernel, first),
        grid_spec=pltpu.PrefetchScalarGridSpec(
            num_scalar_prefetch=2,
            grid=(steps,),
            in_specs=[spec] + [pl.BlockSpec(memory_space=TABLES)] * len(tables),
            out_specs=pl.BlockSpec((BLOCK, width), lambda i, *_: (i, 0)),
            scratch_shapes=[
                pltpu.VMEM((2, CHOSEN * BLOCK, HEAD), jnp.bfloat16),
                pltpu.VMEM((2, CHOSEN * BLOCK, 2 * HEAD), jnp.bfloat16),
                pltpu.SemaphoreType.DMA((2,)),
            ],
        ),
        out_shape=jax.ShapeDtypeStruct((tokens, width), jnp.bfloat16),
        compiler_params=pltpu.CompilerParams(vmem_limit_bytes=VMEM_GRANT),
        cost_estimate=pl.CostEstimate(flops=3 * 10**9, bytes_accessed=8 * 10**6, transcendentals=5 * 10**6),
        name="attend%d" % first,
    )(rows, me, queries, *tables)


def project_kernel(heads_ref, *refs):
    attended, sel_ref, weights = refs[:9], refs[9], refs[10:-8]
    out_ref, acc_ref, a_buf, w_buf, sel_buf, a_sem, w_sem, sel_sem = refs[-8:]
    tokens, width = a_buf.shape[1:]
    groups = [attended[0:2], attended[2:4], attended[4:6], attended[6:]]

    def fetch(r):
        column = pl.multiple_of(heads_ref[r] * width, width)
        start = 0
        for w in weights:
            n = w.shape[0]
            to = w_buf.at[r % 2, pl.ds(start, n), :]
            pltpu.make_async_copy(w.at[:, pl.ds(column, width)], to, w_sem.at[r % 2]).start()
            start += n
        start = 0
        for a in groups[r]:
            n = a.shape[0]
            pltpu.make_async_copy(a, a_buf.at[r, pl.ds(start, n), :], a_sem.at[r]).start()
            start += n

    fetch(0)
    fetch(1)
    pltpu.make_async_copy(sel_ref, sel_buf, sel_sem).start()
    for r in range(4):
        for buffer, sem in ((a_buf.at[r], a_sem.at[r]), (w_buf.at[r % 2], w_sem.at[r % 2])):
            pltpu.make_async_copy(buffer, buffer, sem).wait()
        term = lax.dot_general(
            a_buf[r], w_buf[r % 2], (((1,), (1,)), ((), ())), preferred_element_type=jnp.float32
        )
        if r == 0:
            acc_ref[...] = term
        else:
            acc_ref[...] += term
        if r < 2:
            fetch(r + 2)
    pltpu.make_async_copy(sel_ref, sel_buf, sel_sem).wait()
    out_ref[...] = jnp.dot(
        acc_ref[...].astype(jnp.bfloat16), sel_buf[...], preferred_element_type=jnp.float32
    ).astype(jnp.bfloat16)


def project(heads, attended, weights, sel):
    width = attended[0].shape[1]
    tokens = attended[0].shape[0] + attended[1].shape[0]
    padded = sum(w.shape[0] for w in weights)
    return pl.pallas_call(
        project_kernel,
        in_specs=[pl.BlockSpec(memory_space=pltpu.SMEM)]
        + [pl.BlockSpec(memory_space=pl.ANY)] * (len(attended) + 1 + len(weights)),
        out_specs=pl.BlockSpec(memory_space=pltpu.VMEM),
        scratch_shapes=[
            pltpu.VMEM((tokens, padded), jnp.float32),
            pltpu.VMEM((4, tokens, width), jnp.bfloat16),
            pltpu.VMEM((2, padded, width), jnp.bfloat16),
            pltpu.VMEM(sel.shape, jnp.bfloat16),
            pltpu.SemaphoreType.DMA((4,)),
            pltpu.SemaphoreType.DMA((2,)),
            pltpu.SemaphoreType.DMA,
        ],
        out_shape=jax.ShapeDtypeStruct((tokens, sel.shape[1]), jnp.bfloat16),
        compiler_params=pltpu.CompilerParams(vmem_limit_bytes=VMEM_GRANT),
        cost_estimate=pl.CostEstimate(flops=4 * 10**9, bytes_accessed=14 * 10**6, transcendentals=0),
        name="project",
    )(heads, *attended, sel, *weights)


def unit_sources(me):
    core = me & 1
    z, x = me >> 3, (me >> 1) & 3
    unit = jnp.arange(64)
    dz = jnp.where(unit < 36, unit // 8, (unit - 36) // 8 + 1)
    slot = jnp.where(unit < 36, unit % 8, (unit - 36) % 8)
    holder = jnp.where(unit < 36, core, 1 - core)
    way = 1 - 2 * holder
    from_z = (z - way * dz) & 7
    from_x = (x - way * (slot & 3)) & 3
    return from_z * 8 + from_x * 2 + (holder ^ (slot >> 2))


def per_device(queries, keys, values, selection, out_weight):
    me = lax.axis_index("ctx")
    y = lax.axis_index("head")
    own = join(keys, values)
    other = swap(own)
    columns = out_weight.shape[1]
    own_rows = jnp.pad(out_weight.T, ((0, 16 - columns), (0, 0)))
    n = IN_A * BLOCK
    tables, wz1, w_row = gather(own[:n], other[:n], own[n:], other[n:], own_rows, swap(own_rows))
    blocks_here = keys.shape[0] // BLOCK
    rows = lax.dynamic_slice_in_dim(selection, me * blocks_here, blocks_here, 0)
    heads = jnp.stack([y, (y + 3) % 4, (y + 1) % 4, (y + 2) % 4]).astype(jnp.int32)
    target = unit_sources(me)[:, None] * columns + jnp.arange(16)[None, :]
    target = jnp.where(jnp.arange(16)[None, :] < columns, target, -1).reshape(-1)
    sel = (target[:, None] == jnp.arange(64 * columns)[None, :]).astype(jnp.bfloat16)
    first = attend(rows, me.reshape(1), queries, tables, 0, 2)
    second = attend(after(rows, first, wz1), me.reshape(1), queries, tables, 2, 2)
    up0, down0, wz2 = over_head(first, 1), over_head(first, -1), next_z(after(wz1, first))
    up0, down0 = after(up0, second), after(down0, second)
    up1, down1 = over_head(second, 1), over_head(second, -1)
    wz3 = next_z(after(wz2, up0, down0))
    h = first.shape[0] // 2
    far = [over_head(up0[:h], 1), over_head(down0[h:], -1)]
    wz4 = next_z(after(wz3, up1, down1, *far)[: wz3.shape[0] // 2])
    weights = [w_row, wz1, wz2, wz3, wz4] + [swap(w) for w in (wz1, wz2, wz3, wz4)]
    far.append(over_head(second, 2))
    return project(heads, [first, second, up0, up1, down0, down1, *far], weights, sel)


def solution(mesh):
    placed = (P("ctx", "head"), P("ctx", "head"), P("ctx", "head"), P(), P(None, ("head", "ctx")))
    return jax.shard_map(
        per_device, mesh=mesh, in_specs=placed, out_specs=P("ctx", "head"), check_vma=False
    )
```

```python
import functools
import math

import jax
import jax.numpy as jnp
from jax import lax
from jax.experimental import pallas as pl
from jax.experimental.pallas import tpu as pltpu
from jax.sharding import PartitionSpec as P

HEAD = 128
BLOCK = 128
CHOSEN = 12
BLK_DEV = 4
IN_A = 3
NZ, NX = 8, 4
MASKED = -1e30
TABLES = pl.ANY
VMEM_GRANT = 60 * 1024 * 1024


def along(hop):
    pairs = []
    for z in range(NZ):
        for x in range(NX):
            for c in range(2):
                to_z, to_x, to_c = hop(z, x, c, 1 - 2 * c)
                to = (to_z % NZ) * 2 * NX + (to_x % NX) * 2 + to_c
                pairs.append((z * 2 * NX + x * 2 + c, to))
    return pairs


def next_z(a):
    return lax.ppermute(a, "ctx", along(lambda z, x, c, way: (z + way, x, c)))


def next_x(a):
    return lax.ppermute(a, "ctx", along(lambda z, x, c, way: (z, x + way, c)))


def swap(a):
    return lax.ppermute(a, "ctx", along(lambda z, x, c, way: (z, x, 1 - c)))


def over_head(a, step):
    return lax.ppermute(a, "head", [(i, (i + step) % 4) for i in range(4)])


def join(*parts):
    return jnp.concatenate(parts, axis=0)


def after(a, *others):
    return lax.optimization_barrier((a, *others))[0]


def both_cores(u, mine, theirs, far, far_theirs, own, other):
    same = [own] + [t[:u] for t in mine] + [far] + [t[u:] for t in reversed(theirs)]
    cross = [other] + [t[u:] for t in mine] + [far_theirs] + [t[:u] for t in reversed(theirs)]
    return same, cross


def row_of(x1, x2, swapped, own, other):
    u = own.shape[0]
    same, cross = both_cores(u, [x1], [swapped[: 2 * u]], x2, swapped[2 * u :], own, other)
    return join(*same, *cross)


def gather(a_own, a_other, b_own, b_other, w_own, w_other):
    u, n, v = a_own.shape[0], b_own.shape[0], w_own.shape[0]
    bz1 = next_z(join(b_own, b_other))
    bz1s = swap(bz1)
    bz2 = next_z(bz1)
    ax1 = next_x(after(join(a_own, a_other), bz1))
    wx1 = next_x(after(join(w_own, w_other), bz1))
    near = join(b_own, bz1[:n], bz1s[n:], b_other, bz1[n:], bz1s[:n])
    bz3 = next_z(after(bz2, ax1))
    ax2 = next_x(after(ax1[:u], bz2))
    bx1n = next_x(after(near, bz2))
    row = row_of(ax1, ax2, swap(join(ax1, ax2)), a_own, a_other)
    bz4 = next_z(after(bz3, ax2, wx1)[:n])
    wx2 = next_x(after(wx1, bz3)[:v])
    az1 = next_z(after(row, bz3))
    bx2n = next_x(after(bx1n, bz3)[: 3 * n])
    bzs = swap(join(bz2, bz3, bz4))
    theirs = [bzs[: 2 * n], bzs[2 * n : 4 * n]]
    same, cross = both_cores(n, [bz2, bz3], theirs, bz4, bzs[4 * n :], b_own, b_other)
    rest_same, rest_cross = join(*same[1:]), join(*cross[1:])
    rest_same = after(rest_same, az1, wx2)
    bx1s, az2 = next_x(rest_same), next_z(az1)
    wxs = swap(after(join(wx1, wx2), az1))
    az2, bx1s, bx2n, wxs = lax.optimization_barrier((az2, bx1s, bx2n, wxs))
    bx1c, az3 = next_x(after(rest_cross, az2)), next_z(az2)
    az3, bx1c = lax.optimization_barrier((az3, bx1c))
    bx2r, az4 = next_x(after(bx1s, az3)), next_z(az3[: 4 * u])
    w_row = row_of(wx1, wx2, wxs, w_own, w_other)
    az4s = swap(az4)
    swaps = [swap(t) for t in (az1, az2, az3, bx1n, bx2n, bx1s, bx1c)]
    bx2rs = swap(after(bx2r, az4s, *swaps))
    az1s, az2s, az3s, bx1ns, bx2ns, bx1ss, bx1cs = swaps
    tables = [row, az1, az2, az3, az4, az1s, az2s, az3s, az4s]
    tables += [near, bx1n, bx2n, bx1ns, bx2ns]
    tables += [rest_same, bx1s, bx2r, bx1ss, bx2rs]
    tables += [rest_cross, bx1c, bx1cs]
    return tables, next_z(after(w_row, az4s)), w_row


def relative(me, source, core):
    dz, dx = (me >> 3) - (source >> 3), (me >> 1) - (source >> 1)
    way = 1 - 2 * core
    return (way * dz) & 7, (way * dx) & 3, (source ^ core) & 1


def locate(me, block):
    source, local = block >> 2, block & 3
    core = me & 1
    dz, dx, cross = relative(me, source, core)
    dz_s, dx_s, cross_s = relative(me, source, 1 - core)
    a_mine = (dz < 4) | ((dz == 4) & (cross == 0))
    a_buffer = jnp.where(a_mine, dz, 4 + dz_s)
    a_unit = jnp.where(a_mine, cross * 4 + dx, cross_s * 4 + dx_s)
    b_mine = (dx < 2) | ((dx == 2) & (cross == 0))
    steps = jnp.where(b_mine, dz, dz_s)
    across = jnp.where(b_mine, cross, cross_s)
    hop = jnp.where(b_mine, dx, dx_s)
    near = (steps < 2) | (steps == 7)
    full = jnp.where(b_mine, hop, 2 + hop)
    short = 19 + jnp.where(b_mine, hop, 1 + hop)
    b_buffer = jnp.where(near, 9 + full, jnp.where(across == 0, 14 + full, short))
    b_unit = jnp.where(near, across * 3 + jnp.where(steps == 7, 2, steps), steps - 2)
    a_row, b_row = a_unit * (IN_A * BLOCK), b_unit * ((2 * BLK_DEV - IN_A) * BLOCK)

    def place(piece):
        first = piece < IN_A
        return (
            jnp.where(first, a_buffer, b_buffer),
            jnp.where(first, a_row + piece * BLOCK, b_row + (piece - IN_A) * BLOCK),
        )

    return place(local), place(BLK_DEV + local)


def attend_kernel(first, rows_ref, me_ref, q_ref, *rest):
    tables, (out_ref, k_buf, v_buf, sem) = rest[:22], rest[22:]
    step, steps = pl.program_id(0), pl.num_programs(0)
    me = me_ref[0]

    def fetch(i, slot):
        def one(j, carry):
            block = rows_ref[first + i, j]
            (k_table, k_row), (v_table, v_row) = locate(me, block)
            to = pl.multiple_of(j * BLOCK, BLOCK)
            k_row, v_row = pl.multiple_of(k_row, BLOCK), pl.multiple_of(v_row, BLOCK)
            k_to = k_buf.at[slot, pl.ds(to, BLOCK), :]
            v_to = v_buf.at[slot, pl.ds(to, BLOCK), pl.ds(0, HEAD)]

            def start(table, row, target):
                pltpu.make_async_copy(table.at[pl.ds(row, BLOCK), :], target, sem.at[slot]).start()

            for t, table in enumerate(tables):
                pl.when(k_table == t)(functools.partial(start, table, k_row, k_to))
                pl.when(v_table == t)(functools.partial(start, table, v_row, v_to))
            return carry

        lax.fori_loop(0, CHOSEN, one, 0)

    @pl.when(step == 0)
    def _():
        v_buf[:, :, HEAD:] = jnp.ones((2, CHOSEN * BLOCK, HEAD), jnp.bfloat16)
        fetch(0, 0)

    @pl.when(step + 1 < steps)
    def _():
        fetch(step + 1, (step + 1) & 1)

    slot = step & 1
    own_block = me * rows_ref.shape[0] + first + step
    biases = [None] + [
        jnp.where(rows_ref[first + step, j] == own_block, jnp.float32(MASKED), jnp.float32(0.0))
        for j in range(1, CHOSEN)
    ]
    pltpu.make_async_copy(v_buf.at[slot], v_buf.at[slot], sem.at[slot]).wait()
    token = lax.broadcasted_iota(jnp.int32, (BLOCK, BLOCK), 0)
    key = lax.broadcasted_iota(jnp.int32, (BLOCK, BLOCK), 1)
    causal = key <= token
    factor = jnp.float32(HEAD**-0.5 * math.log2(math.e))
    k_all = k_buf[slot]
    v_all = v_buf[slot]
    for g in range(q_ref.shape[1] // HEAD):
        q = q_ref[:, g * HEAD : (g + 1) * HEAD]
        s = lax.dot_general(q, k_all, (((1,), (1,)), ((), ())), preferred_element_type=jnp.float32)
        parts = [jnp.where(causal, s[:, :BLOCK], MASKED)]
        for j in range(1, CHOSEN):
            parts.append(s[:, j * BLOCK : (j + 1) * BLOCK] + biases[j])
        top = parts[0]
        for part in parts[1:]:
            top = jnp.maximum(top, part)
        peak = jnp.max(top, axis=1, keepdims=True)
        weight = jnp.concatenate(
            [jnp.exp2((part - peak) * factor).astype(jnp.bfloat16) for part in parts], axis=1
        )
        o = jnp.dot(weight, v_all, preferred_element_type=jnp.float32)
        out_ref[:, g * HEAD : (g + 1) * HEAD] = (o[:, :HEAD] / o[:, HEAD:]).astype(jnp.bfloat16)


def attend(rows, me, queries, tables, first, steps):
    width = queries.shape[1]
    tokens = steps * BLOCK
    spec = pl.BlockSpec((BLOCK, width), lambda i, *_: (first + i, 0))
    return pl.pallas_call(
        functools.partial(attend_kernel, first),
        grid_spec=pltpu.PrefetchScalarGridSpec(
            num_scalar_prefetch=2,
            grid=(steps,),
            in_specs=[spec] + [pl.BlockSpec(memory_space=TABLES)] * len(tables),
            out_specs=pl.BlockSpec((BLOCK, width), lambda i, *_: (i, 0)),
            scratch_shapes=[
                pltpu.VMEM((2, CHOSEN * BLOCK, HEAD), jnp.bfloat16),
                pltpu.VMEM((2, CHOSEN * BLOCK, 2 * HEAD), jnp.bfloat16),
                pltpu.SemaphoreType.DMA((2,)),
            ],
        ),
        out_shape=jax.ShapeDtypeStruct((tokens, width), jnp.bfloat16),
        compiler_params=pltpu.CompilerParams(vmem_limit_bytes=VMEM_GRANT),
        cost_estimate=pl.CostEstimate(flops=3 * 10**9, bytes_accessed=8 * 10**6, transcendentals=5 * 10**6),
        name="attend%d" % first,
    )(rows, me, queries, *tables)


def project_kernel(heads_ref, *refs):
    attended, sel_ref, weights = refs[:9], refs[9], refs[10:-8]
    out_ref, acc_ref, a_buf, w_buf, sel_buf, a_sem, w_sem, sel_sem = refs[-8:]
    tokens, width = a_buf.shape[1:]
    groups = [attended[0:2], attended[2:4], attended[4:6], attended[6:]]

    def fetch(r):
        column = pl.multiple_of(heads_ref[r] * width, width)
        start = 0
        for w in weights:
            n = w.shape[0]
            to = w_buf.at[r % 2, pl.ds(start, n), :]
            pltpu.make_async_copy(w.at[:, pl.ds(column, width)], to, w_sem.at[r % 2]).start()
            start += n
        start = 0
        for a in groups[r]:
            n = a.shape[0]
            pltpu.make_async_copy(a, a_buf.at[r, pl.ds(start, n), :], a_sem.at[r]).start()
            start += n

    fetch(0)
    fetch(1)
    pltpu.make_async_copy(sel_ref, sel_buf, sel_sem).start()
    for r in range(4):
        for buffer, sem in ((a_buf.at[r], a_sem.at[r]), (w_buf.at[r % 2], w_sem.at[r % 2])):
            pltpu.make_async_copy(buffer, buffer, sem).wait()
        term = lax.dot_general(
            a_buf[r], w_buf[r % 2], (((1,), (1,)), ((), ())), preferred_element_type=jnp.float32
        )
        if r == 0:
            acc_ref[...] = term
        else:
            acc_ref[...] += term
        if r < 2:
            fetch(r + 2)
    pltpu.make_async_copy(sel_ref, sel_buf, sel_sem).wait()
    out_ref[...] = jnp.dot(
        acc_ref[...].astype(jnp.bfloat16), sel_buf[...], preferred_element_type=jnp.float32
    ).astype(jnp.bfloat16)


def project(heads, attended, weights, sel):
    width = attended[0].shape[1]
    tokens = attended[0].shape[0] + attended[1].shape[0]
    padded = sum(w.shape[0] for w in weights)
    return pl.pallas_call(
        project_kernel,
        in_specs=[pl.BlockSpec(memory_space=pltpu.SMEM)]
        + [pl.BlockSpec(memory_space=pl.ANY)] * (len(attended) + 1 + len(weights)),
        out_specs=pl.BlockSpec(memory_space=pltpu.VMEM),
        scratch_shapes=[
            pltpu.VMEM((tokens, padded), jnp.float32),
            pltpu.VMEM((4, tokens, width), jnp.bfloat16),
            pltpu.VMEM((2, padded, width), jnp.bfloat16),
            pltpu.VMEM(sel.shape, jnp.bfloat16),
            pltpu.SemaphoreType.DMA((4,)),
            pltpu.SemaphoreType.DMA((2,)),
            pltpu.SemaphoreType.DMA,
        ],
        out_shape=jax.ShapeDtypeStruct((tokens, sel.shape[1]), jnp.bfloat16),
        compiler_params=pltpu.CompilerParams(vmem_limit_bytes=VMEM_GRANT),
        cost_estimate=pl.CostEstimate(flops=4 * 10**9, bytes_accessed=14 * 10**6, transcendentals=0),
        name="project",
    )(heads, *attended, sel, *weights)


def unit_sources(me):
    core = me & 1
    z, x = me >> 3, (me >> 1) & 3
    unit = jnp.arange(64)
    dz = jnp.where(unit < 36, unit // 8, (unit - 36) // 8 + 1)
    slot = jnp.where(unit < 36, unit % 8, (unit - 36) % 8)
    holder = jnp.where(unit < 36, core, 1 - core)
    way = 1 - 2 * holder
    from_z = (z - way * dz) & 7
    from_x = (x - way * (slot & 3)) & 3
    return from_z * 8 + from_x * 2 + (holder ^ (slot >> 2))


def per_device(queries, keys, values, selection, out_weight):
    me = lax.axis_index("ctx")
    y = lax.axis_index("head")
    own = join(keys, values)
    other = swap(own)
    columns = out_weight.shape[1]
    own_rows = jnp.pad(out_weight.T, ((0, 16 - columns), (0, 0)))
    n = IN_A * BLOCK
    tables, wz1, w_row = gather(own[:n], other[:n], own[n:], other[n:], own_rows, swap(own_rows))
    blocks_here = keys.shape[0] // BLOCK
    rows = lax.dynamic_slice_in_dim(selection, me * blocks_here, blocks_here, 0)
    heads = jnp.stack([y, (y + 3) % 4, (y + 1) % 4, (y + 2) % 4]).astype(jnp.int32)
    target = unit_sources(me)[:, None] * columns + jnp.arange(16)[None, :]
    target = jnp.where(jnp.arange(16)[None, :] < columns, target, -1).reshape(-1)
    sel = (target[:, None] == jnp.arange(64 * columns)[None, :]).astype(jnp.bfloat16)
    first = attend(rows, me.reshape(1), queries, tables, 0, 2)
    second = attend(after(rows, first, wz1), me.reshape(1), queries, tables, 2, 2)
    up0, down0, wz2 = over_head(first, 1), over_head(first, -1), next_z(after(wz1, first))
    up0, down0 = after(up0, second), after(down0, second)
    up1, down1 = over_head(second, 1), over_head(second, -1)
    wz3 = next_z(after(wz2, up0, down0))
    h = first.shape[0] // 2
    far = [over_head(up0[:h], 1), over_head(down0[h:], -1)]
    wz4 = next_z(after(wz3, up1, down1, *far)[: wz3.shape[0] // 2])
    weights = [w_row, wz1, wz2, wz3, wz4] + [swap(w) for w in (wz1, wz2, wz3, wz4)]
    far.append(over_head(second, 2))
    return project(heads, [first, second, up0, up1, down0, down1, *far], weights, sel)


def solution(mesh):
    placed = (P("ctx", "head"), P("ctx", "head"), P("ctx", "head"), P(), P(None, ("head", "ctx")))
    return jax.shard_map(
        per_device, mesh=mesh, in_specs=placed, out_specs=P("ctx", "head"), check_vma=False
    )
```

```python
import functools
import math

import jax
import jax.numpy as jnp
from jax import lax
from jax.experimental import pallas as pl
from jax.experimental.pallas import tpu as pltpu
from jax.sharding import PartitionSpec as P

HEAD = 128
BLOCK = 128
CHOSEN = 12
BLK_DEV = 4
IN_A = 3
NZ, NX = 8, 4
MASKED = -1e30
TABLES = pl.ANY
VMEM_GRANT = 60 * 1024 * 1024


def along(hop):
    pairs = []
    for z in range(NZ):
        for x in range(NX):
            for c in range(2):
                to_z, to_x, to_c = hop(z, x, c, 1 - 2 * c)
                to = (to_z % NZ) * 2 * NX + (to_x % NX) * 2 + to_c
                pairs.append((z * 2 * NX + x * 2 + c, to))
    return pairs


def next_z(a):
    return lax.ppermute(a, "ctx", along(lambda z, x, c, way: (z + way, x, c)))


def next_x(a):
    return lax.ppermute(a, "ctx", along(lambda z, x, c, way: (z, x + way, c)))


def swap(a):
    return lax.ppermute(a, "ctx", along(lambda z, x, c, way: (z, x, 1 - c)))


def over_head(a, step):
    return lax.ppermute(a, "head", [(i, (i + step) % 4) for i in range(4)])


def join(*parts):
    return jnp.concatenate(parts, axis=0)


def after(a, *others):
    return lax.optimization_barrier((a, *others))[0]


def both_cores(u, mine, theirs, far, far_theirs, own, other):
    same = [own] + [t[:u] for t in mine] + [far] + [t[u:] for t in reversed(theirs)]
    cross = [other] + [t[u:] for t in mine] + [far_theirs] + [t[:u] for t in reversed(theirs)]
    return same, cross


def row_of(x1, x2, swapped, own, other):
    u = own.shape[0]
    same, cross = both_cores(u, [x1], [swapped[: 2 * u]], x2, swapped[2 * u :], own, other)
    return join(*same, *cross)


def gather(a_own, a_other, b_own, b_other, w_own, w_other):
    u, n, v = a_own.shape[0], b_own.shape[0], w_own.shape[0]
    bz1 = next_z(join(b_own, b_other))
    bz1s = swap(bz1)
    bz2 = next_z(bz1)
    ax1 = next_x(after(join(a_own, a_other), bz1))
    wx1 = next_x(after(join(w_own, w_other), bz1))
    near = join(b_own, bz1[:n], bz1s[n:], b_other, bz1[n:], bz1s[:n])
    bz3 = next_z(after(bz2, ax1))
    ax2 = next_x(after(ax1[:u], bz2))
    bx1n = next_x(after(near, bz2))
    row = row_of(ax1, ax2, swap(join(ax1, ax2)), a_own, a_other)
    bz4 = next_z(after(bz3, ax2, wx1)[:n])
    wx2 = next_x(after(wx1, bz3)[:v])
    az1 = next_z(after(row, bz3))
    bx2n = next_x(after(bx1n, bz3)[: 3 * n])
    bzs = swap(join(bz2, bz3, bz4))
    theirs = [bzs[: 2 * n], bzs[2 * n : 4 * n]]
    same, cross = both_cores(n, [bz2, bz3], theirs, bz4, bzs[4 * n :], b_own, b_other)
    rest_same, rest_cross = join(*same[1:]), join(*cross[1:])
    rest_same = after(rest_same, az1, wx2)
    bx1s, az2 = next_x(rest_same), next_z(az1)
    wxs = swap(after(join(wx1, wx2), az1))
    az2, bx1s, bx2n, wxs = lax.optimization_barrier((az2, bx1s, bx2n, wxs))
    bx1c, az3 = next_x(after(rest_cross, az2)), next_z(az2)
    az3, bx1c = lax.optimization_barrier((az3, bx1c))
    bx2r, az4 = next_x(after(bx1s, az3)), next_z(az3[: 4 * u])
    w_row = row_of(wx1, wx2, wxs, w_own, w_other)
    az4s = swap(az4)
    swaps = [swap(t) for t in (az1, az2, az3, bx1n, bx2n, bx1s, bx1c)]
    bx2rs = swap(after(bx2r, az4s, *swaps))
    az1s, az2s, az3s, bx1ns, bx2ns, bx1ss, bx1cs = swaps
    tables = [row, az1, az2, az3, az4, az1s, az2s, az3s, az4s]
    tables += [near, bx1n, bx2n, bx1ns, bx2ns]
    tables += [rest_same, bx1s, bx2r, bx1ss, bx2rs]
    tables += [rest_cross, bx1c, bx1cs]
    return tables, next_z(after(w_row, az4s)), w_row


def relative(me, source, core):
    dz, dx = (me >> 3) - (source >> 3), (me >> 1) - (source >> 1)
    way = 1 - 2 * core
    return (way * dz) & 7, (way * dx) & 3, (source ^ core) & 1


def locate(me, block):
    source, local = block >> 2, block & 3
    core = me & 1
    dz, dx, cross = relative(me, source, core)
    dz_s, dx_s, cross_s = relative(me, source, 1 - core)
    a_mine = (dz < 4) | ((dz == 4) & (cross == 0))
    a_buffer = jnp.where(a_mine, dz, 4 + dz_s)
    a_unit = jnp.where(a_mine, cross * 4 + dx, cross_s * 4 + dx_s)
    b_mine = (dx < 2) | ((dx == 2) & (cross == 0))
    steps = jnp.where(b_mine, dz, dz_s)
    across = jnp.where(b_mine, cross, cross_s)
    hop = jnp.where(b_mine, dx, dx_s)
    near = (steps < 2) | (steps == 7)
    full = jnp.where(b_mine, hop, 2 + hop)
    short = 19 + jnp.where(b_mine, hop, 1 + hop)
    b_buffer = jnp.where(near, 9 + full, jnp.where(across == 0, 14 + full, short))
    b_unit = jnp.where(near, across * 3 + jnp.where(steps == 7, 2, steps), steps - 2)
    a_row, b_row = a_unit * (IN_A * BLOCK), b_unit * ((2 * BLK_DEV - IN_A) * BLOCK)

    def place(piece):
        first = piece < IN_A
        return (
            jnp.where(first, a_buffer, b_buffer),
            jnp.where(first, a_row + piece * BLOCK, b_row + (piece - IN_A) * BLOCK),
        )

    return place(local), place(BLK_DEV + local)


def attend_kernel(first, rows_ref, me_ref, q_ref, *rest):
    tables, (out_ref, k_buf, v_buf, sem) = rest[:22], rest[22:]
    step, steps = pl.program_id(0), pl.num_programs(0)
    me = me_ref[0]

    def fetch(i, slot):
        def one(j, carry):
            block = rows_ref[first + i, j]
            (k_table, k_row), (v_table, v_row) = locate(me, block)
            to = pl.multiple_of(j * BLOCK, BLOCK)
            k_row, v_row = pl.multiple_of(k_row, BLOCK), pl.multiple_of(v_row, BLOCK)
            k_to = k_buf.at[slot, pl.ds(to, BLOCK), :]
            v_to = v_buf.at[slot, pl.ds(to, BLOCK), pl.ds(0, HEAD)]

            def start(table, row, target):
                pltpu.make_async_copy(table.at[pl.ds(row, BLOCK), :], target, sem.at[slot]).start()

            for t, table in enumerate(tables):
                pl.when(k_table == t)(functools.partial(start, table, k_row, k_to))
                pl.when(v_table == t)(functools.partial(start, table, v_row, v_to))
            return carry

        lax.fori_loop(0, CHOSEN, one, 0)

    @pl.when(step == 0)
    def _():
        v_buf[:, :, HEAD:] = jnp.ones((2, CHOSEN * BLOCK, HEAD), jnp.bfloat16)
        fetch(0, 0)

    @pl.when(step + 1 < steps)
    def _():
        fetch(step + 1, (step + 1) & 1)

    slot = step & 1
    own_block = me * rows_ref.shape[0] + first + step
    biases = [None] + [
        jnp.where(rows_ref[first + step, j] == own_block, jnp.float32(MASKED), jnp.float32(0.0))
        for j in range(1, CHOSEN)
    ]
    pltpu.make_async_copy(v_buf.at[slot], v_buf.at[slot], sem.at[slot]).wait()
    token = lax.broadcasted_iota(jnp.int32, (BLOCK, BLOCK), 0)
    key = lax.broadcasted_iota(jnp.int32, (BLOCK, BLOCK), 1)
    causal = key <= token
    factor = jnp.float32(HEAD**-0.5 * math.log2(math.e))
    k_all = k_buf[slot]
    v_all = v_buf[slot]
    for g in range(q_ref.shape[1] // HEAD):
        q = q_ref[:, g * HEAD : (g + 1) * HEAD]
        s = lax.dot_general(q, k_all, (((1,), (1,)), ((), ())), preferred_element_type=jnp.float32)
        parts = [jnp.where(causal, s[:, :BLOCK], MASKED)]
        for j in range(1, CHOSEN):
            parts.append(s[:, j * BLOCK : (j + 1) * BLOCK] + biases[j])
        top = parts[0]
        for part in parts[1:]:
            top = jnp.maximum(top, part)
        peak = jnp.max(top, axis=1, keepdims=True)
        weight = jnp.concatenate(
            [jnp.exp2((part - peak) * factor).astype(jnp.bfloat16) for part in parts], axis=1
        )
        o = jnp.dot(weight, v_all, preferred_element_type=jnp.float32)
        out_ref[:, g * HEAD : (g + 1) * HEAD] = (o[:, :HEAD] / o[:, HEAD:]).astype(jnp.bfloat16)


def attend(rows, me, queries, tables, first, steps):
    width = queries.shape[1]
    tokens = steps * BLOCK
    spec = pl.BlockSpec((BLOCK, width), lambda i, *_: (first + i, 0))
    return pl.pallas_call(
        functools.partial(attend_kernel, first),
        grid_spec=pltpu.PrefetchScalarGridSpec(
            num_scalar_prefetch=2,
            grid=(steps,),
            in_specs=[spec] + [pl.BlockSpec(memory_space=TABLES)] * len(tables),
            out_specs=pl.BlockSpec((BLOCK, width), lambda i, *_: (i, 0)),
            scratch_shapes=[
                pltpu.VMEM((2, CHOSEN * BLOCK, HEAD), jnp.bfloat16),
                pltpu.VMEM((2, CHOSEN * BLOCK, 2 * HEAD), jnp.bfloat16),
                pltpu.SemaphoreType.DMA((2,)),
            ],
        ),
        out_shape=jax.ShapeDtypeStruct((tokens, width), jnp.bfloat16),
        compiler_params=pltpu.CompilerParams(vmem_limit_bytes=VMEM_GRANT),
        cost_estimate=pl.CostEstimate(flops=3 * 10**9, bytes_accessed=8 * 10**6, transcendentals=5 * 10**6),
        name="attend%d" % first,
    )(rows, me, queries, *tables)


def project_kernel(heads_ref, *refs):
    attended, sel_ref, weights = refs[:9], refs[9], refs[10:-8]
    out_ref, acc_ref, a_buf, w_buf, sel_buf, a_sem, w_sem, sel_sem = refs[-8:]
    tokens, width = a_buf.shape[1:]
    groups = [attended[0:2], attended[2:4], attended[4:6], attended[6:]]

    def fetch(r):
        column = pl.multiple_of(heads_ref[r] * width, width)
        start = 0
        for w in weights:
            n = w.shape[0]
            to = w_buf.at[r % 2, pl.ds(start, n), :]
            pltpu.make_async_copy(w.at[:, pl.ds(column, width)], to, w_sem.at[r % 2]).start()
            start += n
        start = 0
        for a in groups[r]:
            n = a.shape[0]
            pltpu.make_async_copy(a, a_buf.at[r, pl.ds(start, n), :], a_sem.at[r]).start()
            start += n

    fetch(0)
    fetch(1)
    for r in range(4):
        for buffer, sem in ((a_buf.at[r], a_sem.at[r]), (w_buf.at[r % 2], w_sem.at[r % 2])):
            pltpu.make_async_copy(buffer, buffer, sem).wait()
        term = lax.dot_general(
            a_buf[r], w_buf[r % 2], (((1,), (1,)), ((), ())), preferred_element_type=jnp.float32
        )
        if r == 0:
            acc_ref[...] = term
        else:
            acc_ref[...] += term
        if r < 2:
            fetch(r + 2)
        if r == 0:
            pltpu.make_async_copy(sel_ref, sel_buf, sel_sem).start()
    pltpu.make_async_copy(sel_ref, sel_buf, sel_sem).wait()
    out_ref[...] = jnp.dot(
        acc_ref[...].astype(jnp.bfloat16), sel_buf[...], preferred_element_type=jnp.float32
    ).astype(jnp.bfloat16)


def project(heads, attended, weights, sel):
    width = attended[0].shape[1]
    tokens = attended[0].shape[0] + attended[1].shape[0]
    padded = sum(w.shape[0] for w in weights)
    return pl.pallas_call(
        project_kernel,
        in_specs=[pl.BlockSpec(memory_space=pltpu.SMEM)]
        + [pl.BlockSpec(memory_space=pl.ANY)] * (len(attended) + 1 + len(weights)),
        out_specs=pl.BlockSpec(memory_space=pltpu.VMEM),
        scratch_shapes=[
            pltpu.VMEM((tokens, padded), jnp.float32),
            pltpu.VMEM((4, tokens, width), jnp.bfloat16),
            pltpu.VMEM((2, padded, width), jnp.bfloat16),
            pltpu.VMEM(sel.shape, jnp.bfloat16),
            pltpu.SemaphoreType.DMA((4,)),
            pltpu.SemaphoreType.DMA((2,)),
            pltpu.SemaphoreType.DMA,
        ],
        out_shape=jax.ShapeDtypeStruct((tokens, sel.shape[1]), jnp.bfloat16),
        compiler_params=pltpu.CompilerParams(vmem_limit_bytes=VMEM_GRANT),
        cost_estimate=pl.CostEstimate(flops=4 * 10**9, bytes_accessed=14 * 10**6, transcendentals=0),
        name="project",
    )(heads, *attended, sel, *weights)


def unit_sources(me):
    core = me & 1
    z, x = me >> 3, (me >> 1) & 3
    unit = jnp.arange(64)
    dz = jnp.where(unit < 36, unit // 8, (unit - 36) // 8 + 1)
    slot = jnp.where(unit < 36, unit % 8, (unit - 36) % 8)
    holder = jnp.where(unit < 36, core, 1 - core)
    way = 1 - 2 * holder
    from_z = (z - way * dz) & 7
    from_x = (x - way * (slot & 3)) & 3
    return from_z * 8 + from_x * 2 + (holder ^ (slot >> 2))


def per_device(queries, keys, values, selection, out_weight):
    me = lax.axis_index("ctx")
    y = lax.axis_index("head")
    own = join(keys, values)
    other = swap(own)
    columns = out_weight.shape[1]
    own_rows = jnp.pad(out_weight.T, ((0, 16 - columns), (0, 0)))
    n = IN_A * BLOCK
    tables, wz1, w_row = gather(own[:n], other[:n], own[n:], other[n:], own_rows, swap(own_rows))
    blocks_here = keys.shape[0] // BLOCK
    rows = lax.dynamic_slice_in_dim(selection, me * blocks_here, blocks_here, 0)
    heads = jnp.stack([y, (y + 3) % 4, (y + 1) % 4, (y + 2) % 4]).astype(jnp.int32)
    target = unit_sources(me)[:, None] * columns + jnp.arange(16)[None, :]
    target = jnp.where(jnp.arange(16)[None, :] < columns, target, -1).reshape(-1)
    sel = (target[:, None] == jnp.arange(64 * columns)[None, :]).astype(jnp.bfloat16)
    first = attend(rows, me.reshape(1), queries, tables, 0, 2)
    second = attend(after(rows, first, wz1), me.reshape(1), queries, tables, 2, 2)
    up0, down0, wz2 = over_head(first, 1), over_head(first, -1), next_z(after(wz1, first))
    up0, down0 = after(up0, second), after(down0, second)
    up1, down1 = over_head(second, 1), over_head(second, -1)
    wz3 = next_z(after(wz2, up0, down0))
    h = first.shape[0] // 2
    far = [over_head(up0[:h], 1), over_head(down0[h:], -1)]
    wz4 = next_z(after(wz3, up1, down1, *far)[: wz3.shape[0] // 2])
    weights = [w_row, wz1, wz2, wz3, wz4] + [swap(w) for w in (wz1, wz2, wz3, wz4)]
    far.append(over_head(second, 2))
    return project(heads, [first, second, up0, up1, down0, down1, *far], weights, sel)


def solution(mesh):
    placed = (P("ctx", "head"), P("ctx", "head"), P("ctx", "head"), P(), P(None, ("head", "ctx")))
    return jax.shard_map(
        per_device, mesh=mesh, in_specs=placed, out_specs=P("ctx", "head"), check_vma=False
    )
```
